32 devices in a mesh: tile: 16 (over z, x, core), agent: 2 (over y).
Axes of the slice: x: 2, y: 2, z: 4, core: 2. Of those that a mesh axis runs over, the one named last changes fastest.
Arguments:
- states: float32 [2, 8, 32, 256], P('agent', None, 'tile'), may hold values from -6 to 6
- footprints: float32 [16, 16, 64, 512], P('agent', 'tile'), may hold values from -0.25 to 0.25
- offsets: int32 [16, 16], P('agent', 'tile'), may hold values from 0 to 1984, as said below
- measured: float32 [16, 8, 2048], P('agent', None, 'tile'), may hold values from -9 to 9
- weights: float32 [16, 8, 2048], P('agent', None, 'tile'), may hold values from 0.2 to 5
Outputs:
- new_states: float32 [2, 8, 32, 256], P('agent', None, 'tile')
- prior_volume: float32 [8, 32, 256], P(None, 'tile')
The draws below stay inside these ranges and needn't reach their ends.
Inputs may be any that keep to these rules, and one draw needn't show every extreme that they name: For one agent and one tile t, the values offsets[v, t] // 128 differ between the agent's 8 views v.
All inputs are finite; a program needn't handle non-finite values.
Results may differ from the reference program's by a relative error of at most 0.0003.
Values sent between devices are 32-bit elements; how exact they have to be, the bound alone decides.
A program may use at most 64 MiB of HBM per device.

```python
import math
import jax
import jax.numpy as jnp
from jax import lax

SL = 8
COLS = 256
V_AG = 8
FOOT = 64
DET = 2048
ITERS = 1
SWEEPS = 2
PIX_DEV = 512
ROWS = 32
AGENTS = 2
TILES = 16
VIEWS = 16


def draw_offsets(key, part):
    share = DET // TILES
    start_count = (DET - FOOT) // share + 1
    score_key = jax.random.fold_in(key, 11)
    shift_key = jax.random.fold_in(key, 23)
    scores = jax.random.randint(score_key, (AGENTS, TILES, start_count), 0, 2 ** 18, dtype=jnp.int32)
    scores = scores * start_count + jnp.arange(start_count, dtype=jnp.int32)[None, None, :]
    order = jnp.argsort(scores, axis=-1, stable=True)[:, :, :V_AG].astype(jnp.int32)
    base = order * share
    upper = jnp.minimum(share, DET - FOOT - base + 1)
    extra = jax.random.randint(shift_key, (AGENTS, TILES, V_AG), 0, upper, dtype=jnp.int32)
    placed = (base + extra).transpose(0, 2, 1)
    return placed.reshape(AGENTS * V_AG, TILES).astype(jnp.int32)


def shard_levels(own_key, dims, shards, smallest, high):
    factor_of = 1.0
    for position, shards_of in shards:
        heights = jax.random.uniform(jax.random.fold_in(jax.random.fold_in(own_key, 6), position), (shards_of,), jnp.float32, smallest / len(shards), high / len(shards))
        factor_of = factor_of * jnp.repeat(jnp.exp(heights), dims[position] // shards_of).reshape((-1,) + (1,) * (len(dims) - 1 - position))
    return factor_of


def bell_draw(rng, extent, deviation, reach, cuts=(), kind=jnp.bfloat16):
    level = shard_levels(rng, extent, cuts, -0.22, 0.18) if cuts else 1.0
    result = jax.random.normal(rng, extent, jnp.float32) * deviation * level
    return jnp.minimum(jnp.maximum(result, -reach), reach).astype(kind)


def setup_inputs(seed: int = 0) -> dict:
    keys = jax.random.split(jax.random.key(seed), 6)
    return {
        "states": bell_draw(keys[0], (AGENTS, SL, ROWS, COLS), 1.0, 6.0, ((0, 2), (2, 16)), jnp.float32),
        "footprints": bell_draw(keys[1], (VIEWS, TILES, FOOT, PIX_DEV), PIX_DEV ** -0.5, 0.25, ((0, 2), (1, 16)), jnp.float32),
        "offsets": draw_offsets(jax.random.fold_in(keys[5], 71), 0),
        "measured": bell_draw(keys[3], (VIEWS, SL, DET), 1.5, 9.0, ((0, 2), (2, 16)), jnp.float32),
        "weights": jnp.clip(jnp.exp(math.log(5.0) - 3.218876 * jax.random.uniform(keys[4], (VIEWS, SL, DET), jnp.float32) ** shard_levels(keys[4], (VIEWS, SL, DET), ((0, 2), (2, 16)), -0.2, 0.2)), 0.2, 5.0),
    }


STEP_SIZE = 0.25
RELAX = 0.6
QRATIO = 0.6


def neighbour_table():
    offsets_nb = []
    for a in (-1, 0, 1):
        for b in (-1, 0, 1):
            for c in (-1, 0, 1):
                if a != 0 or b != 0 or c != 0:
                    offsets_nb.append((a, b, c, 1.0 / ((a * a + b * b + c * c) ** 0.5)))
    total = sum(item[3] for item in offsets_nb)
    return [(a, b, c, 4.0 * w / total) for (a, b, c, w) in offsets_nb]


def sweep_update(padded, average):
    depth, height, width = average.shape
    centre = padded[1:1 + depth, 1:1 + height, 1:1 + width]
    numerator = average
    denominator = jnp.ones_like(average)
    for (a, b, c, weight_nb) in neighbour_table():
        neighbour = padded[1 + a:1 + a + depth, 1 + b:1 + b + height, 1 + c:1 + c + width]
        differ = centre - neighbour
        powered = jnp.power(differ * differ, 0.4)
        coefficient = weight_nb * (1.0 + QRATIO * powered) / ((1.0 + powered) * (1.0 + powered))
        numerator = numerator + coefficient * neighbour
        denominator = denominator + coefficient
    return numerator / denominator


def data_step(packed):
    current, blocks, offsets_ag, measured_ag, weights_ag = packed
    slices = current.shape[0]
    tiles = blocks.shape[1]
    foot = blocks.shape[2]
    pixels = blocks.shape[3]
    detector = measured_ag.shape[2]
    volume = current.reshape(slices, tiles, pixels).transpose(1, 0, 2)
    projected = jnp.einsum('tsp,vtbp->vtbs', volume, blocks, precision=lax.Precision.HIGHEST)
    bin_index = offsets_ag.astype(jnp.int32)[:, :, None] + jnp.arange(foot, dtype=jnp.int32)[None, None, :]

    def place(index_view, values_view):
        empty = jnp.zeros((detector, slices), values_view.dtype)
        return empty.at[index_view.reshape(-1)].add(values_view.reshape(-1, slices))

    sinogram = jax.vmap(place)(bin_index, projected).transpose(0, 2, 1)
    residual = weights_ag * (sinogram - measured_ag)
    residual_t = residual.transpose(0, 2, 1)

    def take(rows_view, index_view):
        return rows_view[index_view]

    windows = jax.vmap(take)(residual_t, bin_index)
    gradient = jnp.einsum('vtbs,vtbp->tsp', windows, blocks, precision=lax.Precision.HIGHEST)
    gradient = gradient.transpose(1, 0, 2).reshape(current.shape)
    return current - STEP_SIZE * gradient


def reference(states, footprints, offsets, measured, weights):
    agents = states.shape[0]
    views = footprints.shape[0] // agents
    blocks = footprints.reshape((agents, views) + footprints.shape[1:])
    offsets_all = offsets.reshape(agents, views, offsets.shape[1])
    measured_all = measured.reshape((agents, views) + measured.shape[1:])
    weights_all = weights.reshape((agents, views) + weights.shape[1:])
    current = states
    prior_vol = states[0]
    for repeat in range(ITERS):
        fitted = lax.map(data_step, (current, blocks, offsets_all, measured_all, weights_all))
        reflect = 2.0 * fitted - current
        average = jnp.sum(reflect, axis=0) / agents
        volume = average
        for sweep_index in range(SWEEPS):
            volume = sweep_update(jnp.pad(volume, 1), average)
        prior_vol = volume
        current = (1.0 - RELAX) * current + RELAX * (2.0 * prior_vol[None] - reflect)
    return current, prior_vol
```

```python
import functools

import jax
import jax.numpy as jnp
from jax import lax
from jax.experimental import pallas as pl
from jax.experimental.pallas import tpu as pltpu
from jax.sharding import PartitionSpec as P

SWEEPS = 2
STEP_SIZE = 0.25
RELAX = 0.6
QRATIO = 0.6
MESH = pl.DeviceIdType.MESH
EXACT = lax.Precision.HIGHEST


def neighbour_table():
    offsets_nb = []
    for a in (-1, 0, 1):
        for b in (-1, 0, 1):
            for c in (-1, 0, 1):
                if a != 0 or b != 0 or c != 0:
                    offsets_nb.append((a, b, c, a * a + b * b + c * c))
    total = sum(1.0 / item[3] ** 0.5 for item in offsets_nb)
    scale = {n: 4.0 / n**0.5 / total for n in (1, 2, 3)}
    return offsets_nb, scale


def shift_zero(value, step, dim):
    if step == 0:
        return value
    size = value.shape[dim]
    index = lax.broadcasted_iota(jnp.int32, value.shape, dim)
    rolled = pltpu.roll(value, (-step) % size, dim)
    inside = index < size - 1 if step == 1 else index >= 1
    return jnp.where(inside, rolled, 0.0)


def sweep_rows(rows, averages):
    offsets_nb, scale = neighbour_table()
    shifted = [
        {(a, c): shift_zero(shift_zero(row, a, 0), c, 1) for a in (-1, 0, 1) for c in (-1, 0, 1)}
        for row in rows
    ]
    result = []
    for r in range(1, len(rows) - 1):
        centre = rows[r]
        num, den = {}, {}
        for a, b, c, kind in offsets_nb:
            neighbour = shifted[r + b][(a, c)]
            differ = centre - neighbour
            powered = jnp.exp(0.4 * jnp.log(differ * differ))
            inverse = 1.0 / (1.0 + powered)
            coefficient = inverse * (QRATIO + (1.0 - QRATIO) * inverse)
            num[kind] = num[kind] + coefficient * neighbour if kind in num else coefficient * neighbour
            den[kind] = den[kind] + coefficient if kind in den else coefficient
        top = averages[r] + sum(scale[n] * num[n] for n in num)
        bottom = 1.0 + sum(scale[n] * den[n] for n in den)
        result.append(top / bottom)
    return result


def each(count, body, first=0):
    if count <= 16:
        for k in range(first, count):
            body(k)
    else:
        lax.fori_loop(first, count, lambda k, c: (body(k), c)[1], 0)


def kernel(
    n_tile, n_agent, states_ref, blocks_hbm, offsets_ref, measured_ref, weights_ref,
    new_ref, prior_ref,
    fp, placed, chosen, acc, fsend, frecv, bsend, brecv, rsend, rrecv,
    fp_sem, fss, frs, bss, brs, rss, rrs,
):
    me, ag = lax.axis_index("tile"), lax.axis_index("agent")
    _, slices, height, width = states_ref.shape
    views, foot, pixels = fp.shape
    share = measured_ref.shape[2]
    pieces = placed.shape[1]
    window = -(-pieces * share // 128) * 128

    blocks_copy = pltpu.make_async_copy(blocks_hbm.at[:, 0], fp, fp_sem)
    blocks_copy.start()

    barrier = pltpu.get_barrier_semaphore()

    def greet(tile, agent):
        pl.semaphore_signal(
            barrier, inc=1, device_id={"tile": tile, "agent": agent}, device_id_type=MESH
        )

    each(n_tile, lambda k: greet(lax.rem(me + k, n_tile), ag), 1)
    has_low, has_high = me > 0, me < n_tile - 1
    for k in range(1, n_agent):
        other = lax.rem(ag + k, n_agent)
        greet(me, other)

        @pl.when(has_low)
        def _():
            greet(me - 1, other)

        @pl.when(has_high)
        def _():
            greet(me + 1, other)

    start = [offsets_ref[v, 0] // share for v in range(views)]
    local = [offsets_ref[v, 0] - start[v] * share for v in range(views)]

    def choose(d):
        for j in range(pieces):
            found = jnp.int32(-1)
            for v in range(views):
                found = jnp.where(start[v] + j == d, v, found)
            chosen[d * pieces + j] = found

    each(n_tile, choose)

    current = [states_ref[0, :, r, :] for r in range(height)]
    volume = jnp.concatenate(current, axis=1)
    blocks_copy.wait()
    matrix = fp[...].reshape(views * foot, pixels)
    projected = lax.dot_general(
        volume, matrix, (((1,), (1,)), ((), ())), precision=EXACT,
        preferred_element_type=jnp.float32,
    )
    for v in range(views):
        block = projected[:, v * foot : (v + 1) * foot]
        block = jnp.concatenate([block, jnp.zeros((slices, window - foot), jnp.float32)], axis=1)
        rolled = pltpu.roll(block, local[v], 1)
        for j in range(pieces):
            placed[v, j] = rolled[:, j * share : (j + 1) * share]

    pl.semaphore_wait(
        barrier,
        n_tile - 1 + (n_agent - 1) * (1 + has_low.astype(jnp.int32) + has_high.astype(jnp.int32)),
    )

    def message(d, ref):
        for j in range(pieces):
            v = chosen[d * pieces + j]
            piece = placed[jnp.maximum(v, 0), j]
            ref[d, j * slices : (j + 1) * slices, :] = jnp.where(v >= 0, piece, 0.0)
            ref[d, pieces * slices + j : pieces * slices + j + 1, :] = jnp.full(
                (1, share), v.astype(jnp.float32)
            )

    def forward(d):
        return pltpu.make_async_remote_copy(
            src_ref=fsend.at[d], dst_ref=frecv.at[me], send_sem=fss.at[d], recv_sem=frs.at[me],
            device_id={"tile": d, "agent": ag}, device_id_type=MESH,
        )

    def forward_from(s):
        return pltpu.make_async_remote_copy(
            src_ref=fsend.at[s], dst_ref=frecv.at[s], send_sem=fss.at[s], recv_sem=frs.at[s],
            device_id={"tile": s, "agent": ag}, device_id_type=MESH,
        )

    def send_forward(k):
        d = lax.rem(me + k, n_tile)
        message(d, fsend)
        forward(d).start()

    each(n_tile, send_forward, 1)
    message(me, frecv)

    acc[...] = -measured_ref[...]

    def gather(k):
        s = lax.rem(me + n_tile - k, n_tile)
        if not (isinstance(k, int) and k == 0):
            forward_from(s).wait_recv()
        for j in range(pieces):
            piece = frecv[s, j * slices : (j + 1) * slices, :]
            label = frecv[s, pieces * slices + j : pieces * slices + j + 1, :]
            label = jnp.broadcast_to(label, piece.shape)
            for v in range(views):
                acc[v] += jnp.where(label == v, piece, 0.0)

    gather(0)
    each(n_tile, gather, 1)

    residual = [weights_ref[v] * acc[v] for v in range(views)]

    def answer(s, ref, row):
        for j in range(pieces):
            label = frecv[s, pieces * slices + j : pieces * slices + j + 1, :]
            label = jnp.broadcast_to(label, (slices, share))
            value = jnp.zeros((slices, share), jnp.float32)
            for v in range(views):
                value = jnp.where(label == v, residual[v], value)
            ref[row, j] = value

    def backward(d):
        return pltpu.make_async_remote_copy(
            src_ref=bsend.at[d], dst_ref=brecv.at[me], send_sem=bss.at[d], recv_sem=brs.at[me],
            device_id={"tile": d, "agent": ag}, device_id_type=MESH,
        )

    def backward_from(s):
        return pltpu.make_async_remote_copy(
            src_ref=bsend.at[s], dst_ref=brecv.at[s], send_sem=bss.at[s], recv_sem=brs.at[s],
            device_id={"tile": s, "agent": ag}, device_id_type=MESH,
        )

    def send_backward(k):
        d = lax.rem(me + k, n_tile)
        answer(d, bsend, d)
        backward(d).start()

    each(n_tile, send_backward, 1)
    answer(me, brecv, me)
    each(n_tile, lambda k: backward_from(lax.rem(me + n_tile - k, n_tile)).wait_recv(), 1)

    windows = []
    for v in range(views):
        parts = [brecv[jnp.minimum(start[v] + j, n_tile - 1), j] for j in range(pieces)]
        if window > pieces * share:
            parts.append(jnp.zeros((slices, window - pieces * share), jnp.float32))
        whole = jnp.concatenate(parts, axis=1)
        windows.append(pltpu.roll(whole, window - local[v], 1)[:, :foot])
    gradient = jnp.dot(
        jnp.concatenate(windows, axis=1), matrix, precision=EXACT,
        preferred_element_type=jnp.float32,
    )
    reflect = volume - (2.0 * STEP_SIZE) * gradient
    rsend[...] = reflect

    def share_copy(agent, step):
        return pltpu.make_async_remote_copy(
            src_ref=rsend, dst_ref=rrecv.at[ag, 1 - step],
            send_sem=rss.at[agent, 1 + step], recv_sem=rrs.at[ag, 1 - step],
            device_id={"tile": me + step, "agent": agent}, device_id_type=MESH,
        )

    def share_from(agent, step):
        return pltpu.make_async_remote_copy(
            src_ref=rsend, dst_ref=rrecv.at[agent, 1 + step],
            send_sem=rss.at[agent, 1 + step], recv_sem=rrs.at[agent, 1 + step],
            device_id={"tile": me + step, "agent": agent}, device_id_type=MESH,
        )

    def sharing(act):
        for k in range(1, n_agent):
            act(lax.rem(ag + k, n_agent), 0)
        for step, there in ((-1, has_low), (1, has_high)):

            @pl.when(there)
            def _():
                for k in range(n_agent):
                    act(lax.rem(ag + k, n_agent), step)

    sharing(lambda agent, step: share_copy(agent, step).start())
    rrecv[ag, 1] = reflect

    @pl.when(jnp.logical_not(has_low))
    def _():
        rrecv[:, 0] = jnp.zeros((n_agent, slices, pixels), jnp.float32)

    @pl.when(jnp.logical_not(has_high))
    def _():
        rrecv[:, 2] = jnp.zeros((n_agent, slices, pixels), jnp.float32)

    sharing(lambda agent, step: share_from(agent, step).wait_recv())

    averages = []
    for spot in range(3):
        total = rrecv[0, spot]
        for a in range(1, n_agent):
            total = total + rrecv[a, spot]
        total = total * (1.0 / n_agent)
        averages += [total[:, r * width : (r + 1) * width] for r in range(height)]
    reach = height - SWEEPS
    averages = averages[reach : len(averages) - reach] if reach else averages
    low = jnp.where(has_low, 1.0, 0.0)
    high = jnp.where(has_high, 1.0, 0.0)
    rows, means = averages, averages
    for sweep in range(SWEEPS):
        rows = sweep_rows(rows, means)
        means = means[1:-1]
        outer = SWEEPS - 1 - sweep
        rows = [
            row * low if i < outer else row * high if i >= len(rows) - outer else row
            for i, row in enumerate(rows)
        ]
    for r in range(height):
        mine = reflect[:, r * width : (r + 1) * width]
        prior_ref[:, r, :] = rows[r]
        new_ref[0, :, r, :] = (1.0 - RELAX) * current[r] + RELAX * (2.0 * rows[r] - mine)

    each(n_tile, lambda k: forward(lax.rem(me + k, n_tile)).wait_send(), 1)
    each(n_tile, lambda k: backward(lax.rem(me + k, n_tile)).wait_send(), 1)
    sharing(lambda agent, step: share_copy(agent, step).wait_send())


def shards(n_tile, n_agent, states, footprints, offsets, measured, weights):
    _, slices, height, width = states.shape
    views, _, foot, pixels = footprints.shape
    share = measured.shape[2]
    pieces = (2 * share + foot - 2) // share
    vmem = pl.BlockSpec(memory_space=pltpu.VMEM)
    rows = pieces * slices + pieces
    f32 = jnp.float32
    return tuple(
        pl.pallas_call(
            functools.partial(kernel, n_tile, n_agent),
            out_shape=(
                jax.ShapeDtypeStruct(states.shape, f32),
                jax.ShapeDtypeStruct(states.shape[1:], f32),
            ),
            in_specs=[
                vmem,
                pl.BlockSpec(memory_space=pl.ANY),
                pl.BlockSpec(memory_space=pltpu.SMEM),
                vmem,
                vmem,
            ],
            out_specs=(vmem, vmem),
            scratch_shapes=[
                pltpu.VMEM((views, foot, pixels), f32),
                pltpu.VMEM((views, pieces, slices, share), f32),
                pltpu.SMEM((n_tile * pieces,), jnp.int32),
                pltpu.VMEM((views, slices, share), f32),
                pltpu.VMEM((n_tile, rows, share), f32),
                pltpu.VMEM((n_tile, rows, share), f32),
                pltpu.VMEM((n_tile, pieces, slices, share), f32),
                pltpu.VMEM((n_tile, pieces, slices, share), f32),
                pltpu.VMEM((slices, pixels), f32),
                pltpu.VMEM((n_agent, 3, slices, pixels), f32),
                pltpu.SemaphoreType.DMA,
                pltpu.SemaphoreType.DMA((n_tile,)),
                pltpu.SemaphoreType.DMA((n_tile,)),
                pltpu.SemaphoreType.DMA((n_tile,)),
                pltpu.SemaphoreType.DMA((n_tile,)),
                pltpu.SemaphoreType.DMA((n_agent, 3)),
                pltpu.SemaphoreType.DMA((n_agent, 3)),
            ],
            compiler_params=pltpu.CompilerParams(
                collective_id=0, has_side_effects=True, vmem_limit_bytes=32 * 2**20
            ),
        )(states, footprints, offsets, measured, weights)
    )


def solution(mesh):
    in_specs = (
        P("agent", None, "tile", None),
        P("agent", "tile", None, None),
        P("agent", "tile"),
        P("agent", None, "tile"),
        P("agent", None, "tile"),
    )
    out_specs = (P("agent", None, "tile", None), P(None, "tile", None))
    body = functools.partial(shards, mesh.shape["tile"], mesh.shape["agent"])
    return jax.shard_map(body, mesh=mesh, in_specs=in_specs, out_specs=out_specs, check_vma=False)
```

```python
import functools

import jax
import jax.numpy as jnp
from jax import lax
from jax.experimental import pallas as pl
from jax.experimental.pallas import tpu as pltpu
from jax.sharding import PartitionSpec as P

SWEEPS = 2
STEP_SIZE = 0.25
RELAX = 0.6
QRATIO = 0.6
MESH = pl.DeviceIdType.MESH


def neighbour_table():
    offsets_nb = []
    for a in (-1, 0, 1):
        for b in (-1, 0, 1):
            for c in (-1, 0, 1):
                if a != 0 or b != 0 or c != 0:
                    offsets_nb.append((a, b, c, a * a + b * b + c * c))
    total = sum(1.0 / item[3] ** 0.5 for item in offsets_nb)
    scale = {n: 4.0 / n**0.5 / total for n in (1, 2, 3)}
    return offsets_nb, scale


def shift_zero(value, step, dim):
    if step == 0:
        return value
    size = value.shape[dim]
    index = lax.broadcasted_iota(jnp.int32, value.shape, dim)
    rolled = pltpu.roll(value, (-step) % size, dim)
    inside = index < size - 1 if step == 1 else index >= 1
    return jnp.where(inside, rolled, 0.0)


def sweep_rows(rows, averages):
    offsets_nb, scale = neighbour_table()
    shifted = [
        {(a, c): shift_zero(shift_zero(row, a, 0), c, 1) for a in (-1, 0, 1) for c in (-1, 0, 1)}
        for row in rows
    ]
    result = []
    for r in range(1, len(rows) - 1):
        centre = rows[r]
        num, den = {}, {}
        for a, b, c, kind in offsets_nb:
            neighbour = shifted[r + b][(a, c)]
            differ = centre - neighbour
            powered = jnp.exp(0.4 * jnp.log(differ * differ))
            inverse = pl.reciprocal(1.0 + powered, approx=True)
            coefficient = inverse * (QRATIO + (1.0 - QRATIO) * inverse)
            num[kind] = num[kind] + coefficient * neighbour if kind in num else coefficient * neighbour
            den[kind] = den[kind] + coefficient if kind in den else coefficient
        top = averages[r] + sum(scale[n] * num[n] for n in num)
        bottom = 1.0 + sum(scale[n] * den[n] for n in den)
        result.append(top / bottom)
    return result


def each(count, body, first=0):
    if count <= 16:
        for k in range(first, count):
            body(k)
    else:
        lax.fori_loop(first, count, lambda k, c: (body(k), c)[1], 0)


def split(value):
    high = value.astype(jnp.bfloat16)
    return high, (value - high.astype(jnp.float32)).astype(jnp.bfloat16)


def lanes(rows, count):
    return lax.broadcasted_iota(jnp.int32, (rows, count), 1)


class Windows:
    def __init__(self, slices, views, foot, share):
        self.slices, self.views, self.foot, self.share = slices, views, foot, share
        self.pieces = (2 * share + foot - 2) // share
        self.width = -(-self.pieces * share // 128) * 128
        self.rows = self.pieces * slices + self.pieces
        self.placed_shape = (self.pieces, slices, share)
        self.back_shape = (self.pieces * slices, share)

    def place(self, block, shift):
        zeros = jnp.zeros((self.slices, self.width - self.foot), jnp.float32)
        rolled = pltpu.roll(jnp.concatenate([block, zeros], axis=1), shift, 1)
        share = self.share
        return jnp.stack([rolled[:, j * share : (j + 1) * share] for j in range(self.pieces)])

    def pack(self, views, shifts, placed):
        parts = [placed[v, j] for j, v in enumerate(views)]
        parts += [jnp.full((1, self.share), v.astype(jnp.float32)) for v in views]
        return jnp.concatenate(parts, axis=0)

    def labels(self, packed):
        base = self.pieces * self.slices
        shape = (self.slices, self.share)
        return [jnp.broadcast_to(packed[base + j : base + j + 1], shape) for j in range(self.pieces)]

    def values(self, packed):
        return [packed[j * self.slices : (j + 1) * self.slices] for j in range(self.pieces)]

    def answer(self, values):
        return jnp.concatenate(values, axis=0)

    def window(self, load, shift):
        parts = [load(j)[j * self.slices : (j + 1) * self.slices] for j in range(self.pieces)]
        rest = self.width - self.pieces * self.share
        if rest:
            parts.append(jnp.zeros((self.slices, rest), jnp.float32))
        whole = jnp.concatenate(parts, axis=1)
        return pltpu.roll(whole, self.width - shift, 1)[:, : self.foot]


class Folded:
    pieces = 2

    def __init__(self, slices, views, foot, share):
        self.slices, self.views, self.foot, self.share = slices, views, foot, share
        self.rows = slices + 2
        self.placed_shape = (1, slices, share)
        self.back_shape = (slices, share)

    def halves(self):
        lane = lanes(self.slices, self.share)
        return lane, lane < self.foot

    def place(self, block, shift):
        lane, lower = self.halves()
        rolled = pltpu.roll(jnp.concatenate([block, block], axis=1), shift, 1)
        spill = shift - self.foot
        slack = jnp.where(lower, spill - 1 - lane, lane - self.foot - spill)
        return jnp.where(slack >= 0, rolled, 0.0)[None]

    def pack(self, views, shifts, placed):
        _, lower = self.halves()
        lane = lanes(1, self.share)
        body = jnp.where(lower, placed[views[1], 0], placed[views[0], 0])
        none = jnp.float32(self.views)
        first = (lane >= shifts[0]) & (lane < shifts[0] + self.foot)
        first = jnp.where(first, views[0].astype(jnp.float32), none)
        second = jnp.where(lane < shifts[1] - self.foot, views[1].astype(jnp.float32), none)
        return jnp.concatenate([body, first, second], axis=0)

    def labels(self, packed):
        shape = (self.slices, self.share)
        base = self.slices
        return [jnp.broadcast_to(packed[base + j : base + j + 1], shape) for j in range(2)]

    def values(self, packed):
        _, lower = self.halves()
        body = packed[: self.slices]
        return [jnp.where(lower, pltpu.roll(body, self.foot, 1), body), body]

    def answer(self, values):
        _, lower = self.halves()
        return jnp.where(lower, values[1], values[0] + pltpu.roll(values[0], self.foot, 1))

    def window(self, load, shift):
        lane, lower = self.halves()
        first, second = load(0), load(1)
        first = jnp.where(lower, pltpu.roll(first, self.foot, 1), first)
        second = jnp.where(lower, second, pltpu.roll(second, self.foot, 1))
        residue = jnp.where(lower, lane, lane - self.foot)
        both = jnp.where(residue < shift - self.foot, second, first)
        return pltpu.roll(both, self.share - shift, 1)[:, : self.foot]


def kernel(
    n_tile, n_agent, form, states_hbm, blocks_hbm, offsets_hbm, measured_hbm, weights_hbm,
    average_ref, base_ref,
    states_ref, fp, offsets_ref, measured_ref, weights_ref,
    fp_high, fp_low, placed, chosen, fsend, frecv, bsend, brecv, rsend, rrecv,
    load_sem, fss, frs, bss, brs, rss, rrs,
):
    me, ag = lax.axis_index("tile"), lax.axis_index("agent")
    slices, height, width = states_ref.shape
    views, foot, pixels = fp.shape
    share = measured_ref.shape[2]
    pieces = form.pieces

    loads = [
        pltpu.make_async_copy(source, target, load_sem.at[i])
        for i, (source, target) in enumerate(
            [
                (offsets_hbm, offsets_ref),
                (states_hbm.at[0], states_ref),
                (blocks_hbm.at[:, 0], fp),
                (measured_hbm, measured_ref),
                (weights_hbm, weights_ref),
            ]
        )
    ]
    for copy in loads:
        copy.start()

    barrier = pltpu.get_barrier_semaphore()

    def greet(tile, agent):
        pl.semaphore_signal(
            barrier, inc=1, device_id={"tile": tile, "agent": agent}, device_id_type=MESH
        )

    each(n_tile, lambda k: greet(lax.rem(me + k, n_tile), ag), 1)
    has_low, has_high = me > 0, me < n_tile - 1
    for k in range(1, n_agent):
        other = lax.rem(ag + k, n_agent)
        greet(me, other)

        @pl.when(has_low)
        def _():
            greet(me - 1, other)

        @pl.when(has_high)
        def _():
            greet(me + 1, other)

    loads[0].wait()
    start = [offsets_ref[0, v] // share for v in range(views)]
    local = [offsets_ref[0, v] - start[v] * share for v in range(views)]

    def choose(d):
        for j in range(pieces):
            found, shift = jnp.int32(views), jnp.int32(0)
            for v in range(views):
                hit = start[v] + j == d
                found = jnp.where(hit, v, found)
                shift = jnp.where(hit, local[v], shift)
            chosen[0, d * pieces + j] = found
            chosen[1, d * pieces + j] = shift

    each(n_tile, choose)
    placed[views] = jnp.zeros(form.placed_shape, jnp.float32)

    loads[1].wait()
    current = [states_ref[:, r, :] for r in range(height)]
    volume = jnp.concatenate(current, axis=1)
    volume_both = jnp.concatenate(split(volume), axis=0)
    loads[2].wait()
    for v in range(views):
        fp_high[v * foot : (v + 1) * foot], fp_low[v * foot : (v + 1) * foot] = split(fp[v])

    def product(left, right):
        return lax.dot_general(
            left, right, (((1,), (1,)), ((), ())), preferred_element_type=jnp.float32
        )

    parts = product(fp_high[...], volume_both)
    extra = product(fp_low[...], volume_both)
    parts = jnp.transpose(parts + jnp.where(lanes(*extra.shape) < slices, extra, 0.0))
    projected = parts[:slices] + parts[slices:]
    for v in range(views):
        placed[v] = form.place(projected[:, v * foot : (v + 1) * foot], local[v])

    pl.semaphore_wait(
        barrier,
        n_tile - 1 + (n_agent - 1) * (1 + has_low.astype(jnp.int32) + has_high.astype(jnp.int32)),
    )

    def message(d):
        spots = [d * pieces + j for j in range(pieces)]
        return form.pack([chosen[0, i] for i in spots], [chosen[1, i] for i in spots], placed)

    def forward(d):
        return pltpu.make_async_remote_copy(
            src_ref=fsend.at[d], dst_ref=frecv.at[me], send_sem=fss.at[d], recv_sem=frs.at[me],
            device_id={"tile": d, "agent": ag}, device_id_type=MESH,
        )

    def forward_from(s):
        return pltpu.make_async_remote_copy(
            src_ref=fsend.at[s], dst_ref=frecv.at[s], send_sem=fss.at[s], recv_sem=frs.at[s],
            device_id={"tile": s, "agent": ag}, device_id_type=MESH,
        )

    def send_forward(k):
        d = lax.rem(me + k, n_tile)
        fsend[d] = message(d)
        forward(d).start()

    each(n_tile, send_forward, 1)
    frecv[me] = message(me)

    loads[3].wait()
    loads[4].wait()

    def add(sums, s):
        packed = frecv[s]
        for label, value in zip(form.labels(packed), form.values(packed)):
            sums = [old + jnp.where(label == v, value, 0.0) for v, old in enumerate(sums)]
        return tuple(sums)

    def gather(k, sums):
        s = lax.rem(me + n_tile - k, n_tile)
        forward_from(s).wait_recv()
        return add(sums, s)

    sums = add([-measured_ref[v] for v in range(views)], me)
    sums = lax.fori_loop(1, n_tile, gather, sums, unroll=n_tile <= 16)
    residual = [weights_ref[v] * sums[v] for v in range(views)]

    def answer(s):
        values = []
        for label in form.labels(frecv[s]):
            value = jnp.zeros((slices, share), jnp.float32)
            for v in range(views):
                value = jnp.where(label == v, residual[v], value)
            values.append(value)
        return form.answer(values)

    def backward(d):
        return pltpu.make_async_remote_copy(
            src_ref=bsend.at[d], dst_ref=brecv.at[me], send_sem=bss.at[d], recv_sem=brs.at[me],
            device_id={"tile": d, "agent": ag}, device_id_type=MESH,
        )

    def backward_from(s):
        return pltpu.make_async_remote_copy(
            src_ref=bsend.at[s], dst_ref=brecv.at[s], send_sem=bss.at[s], recv_sem=brs.at[s],
            device_id={"tile": s, "agent": ag}, device_id_type=MESH,
        )

    def send_backward(k):
        d = lax.rem(me + k, n_tile)
        bsend[d] = answer(d)
        backward(d).start()

    each(n_tile, send_backward, 1)
    brecv[me] = answer(me)
    each(n_tile, lambda k: backward_from(lax.rem(me + n_tile - k, n_tile)).wait_recv(), 1)

    windows = [
        form.window(lambda j: brecv[jnp.minimum(start[v] + j, n_tile - 1)], local[v])
        for v in range(views)
    ]
    high, low = split(jnp.concatenate(windows, axis=1))
    both = jnp.dot(
        jnp.concatenate([high, low], axis=0), fp_high[...], preferred_element_type=jnp.float32
    )
    gradient = both[:slices] + both[slices:]
    gradient += jnp.dot(high, fp_low[...], preferred_element_type=jnp.float32)
    reflect = volume - (2.0 * STEP_SIZE) * gradient
    rsend[...] = reflect

    def share_copy(agent, step):
        return pltpu.make_async_remote_copy(
            src_ref=rsend, dst_ref=rrecv.at[ag, 1 - step],
            send_sem=rss.at[agent, 1 + step], recv_sem=rrs.at[ag, 1 - step],
            device_id={"tile": me + step, "agent": agent}, device_id_type=MESH,
        )

    def share_from(agent, step):
        return pltpu.make_async_remote_copy(
            src_ref=rsend, dst_ref=rrecv.at[agent, 1 + step],
            send_sem=rss.at[agent, 1 + step], recv_sem=rrs.at[agent, 1 + step],
            device_id={"tile": me + step, "agent": agent}, device_id_type=MESH,
        )

    def sharing(act):
        for k in range(1, n_agent):
            act(lax.rem(ag + k, n_agent), 0)
        for step, there in ((-1, has_low), (1, has_high)):

            @pl.when(there)
            def _():
                for k in range(n_agent):
                    act(lax.rem(ag + k, n_agent), step)

    sharing(lambda agent, step: share_copy(agent, step).start())
    rrecv[ag, 1] = reflect

    @pl.when(jnp.logical_not(has_low))
    def _():
        rrecv[:, 0] = jnp.zeros((n_agent, slices, pixels), jnp.float32)

    @pl.when(jnp.logical_not(has_high))
    def _():
        rrecv[:, 2] = jnp.zeros((n_agent, slices, pixels), jnp.float32)

    for r in range(height):
        mine = reflect[:, r * width : (r + 1) * width]
        base_ref[r] = (1.0 - RELAX) * current[r] - RELAX * mine

    each(n_tile, lambda k: forward(lax.rem(me + k, n_tile)).wait_send(), 1)
    each(n_tile, lambda k: backward(lax.rem(me + k, n_tile)).wait_send(), 1)
    sharing(lambda agent, step: share_from(agent, step).wait_recv())

    for spot in range(3):
        total = rrecv[0, spot]
        for a in range(1, n_agent):
            total = total + rrecv[a, spot]
        total = total * (1.0 / n_agent)
        for r in range(height):
            average_ref[spot * height + r] = total[:, r * width : (r + 1) * width]
    sharing(lambda agent, step: share_copy(agent, step).wait_send())


def prior_kernel(n_tile, average_ref, base_ref, new_ref, prior_ref):
    me = lax.axis_index("tile")
    height = base_ref.shape[0]
    reach = height - SWEEPS
    rows = [average_ref[i] for i in range(reach, 3 * height - reach)]
    low = jnp.where(me > 0, 1.0, 0.0)
    high = jnp.where(me < n_tile - 1, 1.0, 0.0)
    means = rows
    for sweep in range(SWEEPS):
        rows = sweep_rows(rows, means)
        means = means[1:-1]
        outer = SWEEPS - 1 - sweep
        rows = [
            row * low if i < outer else row * high if i >= len(rows) - outer else row
            for i, row in enumerate(rows)
        ]
    for r in range(height):
        prior_ref[:, r, :] = rows[r]
        new_ref[0, :, r, :] = base_ref[r] + (2.0 * RELAX) * rows[r]


def shards(n_tile, n_agent, states, footprints, offsets, measured, weights):
    _, slices, height, width = states.shape
    views, _, foot, pixels = footprints.shape
    share = measured.shape[2]
    fold = share == 2 * foot and share % 128 == 0
    form = (Folded if fold else Windows)(slices, views, foot, share)
    vmem = pl.BlockSpec(memory_space=pltpu.VMEM)
    hbm = pl.BlockSpec(memory_space=pltpu.HBM)
    f32 = jnp.float32
    dma = pltpu.SemaphoreType.DMA
    average, base = pl.pallas_call(
        functools.partial(kernel, n_tile, n_agent, form),
        out_shape=(
            jax.ShapeDtypeStruct((3 * height, slices, width), f32),
            jax.ShapeDtypeStruct((height, slices, width), f32),
        ),
        in_specs=[hbm] * 5,
        out_specs=(vmem, vmem),
        scratch_shapes=[
            pltpu.VMEM((slices, height, width), f32),
            pltpu.VMEM((views, foot, pixels), f32),
            pltpu.SMEM((1, views), jnp.int32),
            pltpu.VMEM(measured.shape, f32),
            pltpu.VMEM(weights.shape, f32),
            pltpu.VMEM((views * foot, pixels), jnp.bfloat16),
            pltpu.VMEM((views * foot, pixels), jnp.bfloat16),
            pltpu.VMEM((views + 1,) + form.placed_shape, f32),
            pltpu.SMEM((2, n_tile * form.pieces), jnp.int32),
            pltpu.VMEM((n_tile, form.rows, share), f32),
            pltpu.VMEM((n_tile, form.rows, share), f32),
            pltpu.VMEM((n_tile,) + form.back_shape, f32),
            pltpu.VMEM((n_tile,) + form.back_shape, f32),
            pltpu.VMEM((slices, pixels), f32),
            pltpu.VMEM((n_agent, 3, slices, pixels), f32),
            dma((5,)),
            dma((n_tile,)),
            dma((n_tile,)),
            dma((n_tile,)),
            dma((n_tile,)),
            dma((n_agent, 3)),
            dma((n_agent, 3)),
        ],
        compiler_params=pltpu.CompilerParams(
            collective_id=0, has_side_effects=True, vmem_limit_bytes=60 * 2**20
        ),
    )(states, footprints, offsets.reshape(1, views), measured, weights)
    return tuple(
        pl.pallas_call(
            functools.partial(prior_kernel, n_tile),
            out_shape=(
                jax.ShapeDtypeStruct(states.shape, f32),
                jax.ShapeDtypeStruct(states.shape[1:], f32),
            ),
            in_specs=[vmem, vmem],
            out_specs=(vmem, vmem),
            compiler_params=pltpu.CompilerParams(vmem_limit_bytes=60 * 2**20),
        )(average, base)
    )


def solution(mesh):
    in_specs = (
        P("agent", None, "tile", None),
        P("agent", "tile", None, None),
        P("agent", "tile"),
        P("agent", None, "tile"),
        P("agent", None, "tile"),
    )
    out_specs = (P("agent", None, "tile", None), P(None, "tile", None))
    body = functools.partial(shards, mesh.shape["tile"], mesh.shape["agent"])
    return jax.shard_map(body, mesh=mesh, in_specs=in_specs, out_specs=out_specs, check_vma=False)
```

```python
import functools

import jax
import jax.numpy as jnp
from jax import lax
from jax.experimental import pallas as pl
from jax.experimental.pallas import tpu as pltpu
from jax.sharding import PartitionSpec as P

SWEEPS = 2
STEP_SIZE = 0.25
RELAX = 0.6
QRATIO = 0.6
MESH = pl.DeviceIdType.MESH


def neighbour_table():
    offsets_nb = []
    for a in (-1, 0, 1):
        for b in (-1, 0, 1):
            for c in (-1, 0, 1):
                if a != 0 or b != 0 or c != 0:
                    offsets_nb.append((a, b, c, a * a + b * b + c * c))
    total = sum(1.0 / item[3] ** 0.5 for item in offsets_nb)
    scale = {n: 4.0 / n**0.5 / total for n in (1, 2, 3)}
    return offsets_nb, scale


def shift_zero(value, step, dim):
    if step == 0:
        return value
    size = value.shape[dim]
    index = lax.broadcasted_iota(jnp.int32, value.shape, dim)
    rolled = pltpu.roll(value, (-step) % size, dim)
    inside = index < size - 1 if step == 1 else index >= 1
    return jnp.where(inside, rolled, 0.0)


def sweep_rows(rows, averages):
    offsets_nb, scale = neighbour_table()
    shifted = [
        {(a, c): shift_zero(shift_zero(row, a, 0), c, 1) for a in (-1, 0, 1) for c in (-1, 0, 1)}
        for row in rows
    ]
    result = []
    for r in range(1, len(rows) - 1):
        centre = rows[r]
        num, den = {}, {}
        for a, b, c, kind in offsets_nb:
            neighbour = shifted[r + b][(a, c)]
            differ = centre - neighbour
            powered = jnp.exp(0.4 * jnp.log(differ * differ))
            inverse = pl.reciprocal(1.0 + powered, approx=True)
            coefficient = inverse * (QRATIO + (1.0 - QRATIO) * inverse)
            num[kind] = num[kind] + coefficient * neighbour if kind in num else coefficient * neighbour
            den[kind] = den[kind] + coefficient if kind in den else coefficient
        top = averages[r] + sum(scale[n] * num[n] for n in num)
        bottom = 1.0 + sum(scale[n] * den[n] for n in den)
        result.append(top / bottom)
    return result


def far_first(count):
    return sorted(range(1, count), key=lambda k: -min(k, count - k))


def each(count, body, first=0):
    if count <= 16:
        for k in far_first(count) if first else range(count):
            body(k)
    else:
        lax.fori_loop(first, count, lambda k, c: (body(k), c)[1], 0)


def split(value):
    high = value.astype(jnp.bfloat16)
    return high, (value - high.astype(jnp.float32)).astype(jnp.bfloat16)


def lanes(rows, count):
    return lax.broadcasted_iota(jnp.int32, (rows, count), 1)


class Windows:
    def __init__(self, slices, views, foot, share):
        self.slices, self.views, self.foot, self.share = slices, views, foot, share
        self.pieces = (2 * share + foot - 2) // share
        self.width = -(-self.pieces * share // 128) * 128
        self.rows = self.pieces * slices + self.pieces
        self.placed_shape = (self.pieces, slices, share)
        self.back_shape = (self.pieces * slices, share)

    def place(self, block, shift):
        zeros = jnp.zeros((self.slices, self.width - self.foot), jnp.float32)
        rolled = pltpu.roll(jnp.concatenate([block, zeros], axis=1), shift, 1)
        share = self.share
        return jnp.stack([rolled[:, j * share : (j + 1) * share] for j in range(self.pieces)])

    def pack(self, views, shifts, placed):
        parts = [placed[v, j] for j, v in enumerate(views)]
        parts += [jnp.full((1, self.share), v.astype(jnp.float32)) for v in views]
        return jnp.concatenate(parts, axis=0)

    def labels(self, packed):
        base = self.pieces * self.slices
        shape = (self.slices, self.share)
        return [jnp.broadcast_to(packed[base + j : base + j + 1], shape) for j in range(self.pieces)]

    def values(self, packed):
        return [packed[j * self.slices : (j + 1) * self.slices] for j in range(self.pieces)]

    def answer(self, values):
        return jnp.concatenate(values, axis=0)

    def window(self, load, shift):
        parts = [load(j)[j * self.slices : (j + 1) * self.slices] for j in range(self.pieces)]
        rest = self.width - self.pieces * self.share
        if rest:
            parts.append(jnp.zeros((self.slices, rest), jnp.float32))
        whole = jnp.concatenate(parts, axis=1)
        return pltpu.roll(whole, self.width - shift, 1)[:, : self.foot]


class Folded:
    pieces = 2

    def __init__(self, slices, views, foot, share):
        self.slices, self.views, self.foot, self.share = slices, views, foot, share
        self.rows = slices + 2
        self.placed_shape = (1, slices, share)
        self.back_shape = (slices, share)

    def halves(self):
        lane = lanes(self.slices, self.share)
        return lane, lane < self.foot

    def place(self, block, shift):
        lane, lower = self.halves()
        rolled = pltpu.roll(jnp.concatenate([block, block], axis=1), shift, 1)
        spill = shift - self.foot
        slack = jnp.where(lower, spill - 1 - lane, lane - self.foot - spill)
        return jnp.where(slack >= 0, rolled, 0.0)[None]

    def pack(self, views, shifts, placed):
        _, lower = self.halves()
        lane = lanes(1, self.share)
        body = jnp.where(lower, placed[views[1], 0], placed[views[0], 0])
        none = jnp.float32(self.views)
        first = (lane >= shifts[0]) & (lane < shifts[0] + self.foot)
        first = jnp.where(first, views[0].astype(jnp.float32), none)
        second = jnp.where(lane < shifts[1] - self.foot, views[1].astype(jnp.float32), none)
        return jnp.concatenate([body, first, second], axis=0)

    def labels(self, packed):
        shape = (self.slices, self.share)
        base = self.slices
        return [jnp.broadcast_to(packed[base + j : base + j + 1], shape) for j in range(2)]

    def values(self, packed):
        _, lower = self.halves()
        body = packed[: self.slices]
        return [jnp.where(lower, pltpu.roll(body, self.foot, 1), body), body]

    def answer(self, values):
        _, lower = self.halves()
        return jnp.where(lower, values[1], values[0] + pltpu.roll(values[0], self.foot, 1))

    def window(self, load, shift):
        lane, lower = self.halves()
        first, second = load(0), load(1)
        first = jnp.where(lower, pltpu.roll(first, self.foot, 1), first)
        second = jnp.where(lower, second, pltpu.roll(second, self.foot, 1))
        residue = jnp.where(lower, lane, lane - self.foot)
        both = jnp.where(residue < shift - self.foot, second, first)
        return pltpu.roll(both, self.share - shift, 1)[:, : self.foot]


def kernel(
    n_tile, n_agent, form, states_hbm, blocks_hbm, offsets_hbm, measured_hbm, weights_hbm,
    average_ref, base_ref,
    states_ref, fp, offsets_ref, measured_ref, weights_ref,
    fp_high, fp_low, placed, chosen, fsend, frecv, bsend, brecv, rsend, rrecv,
    load_sem, fss, frs, bss, brs, rss, rrs,
):
    me, ag = lax.axis_index("tile"), lax.axis_index("agent")
    slices, height, width = states_ref.shape
    views, foot, pixels = fp.shape
    share = measured_ref.shape[2]
    pieces = form.pieces

    loads = [
        pltpu.make_async_copy(source, target, load_sem.at[i])
        for i, (source, target) in enumerate(
            [
                (offsets_hbm, offsets_ref),
                (states_hbm.at[0], states_ref),
                (measured_hbm, measured_ref),
                (weights_hbm, weights_ref),
            ]
            + [(blocks_hbm.at[v, 0], fp.at[v]) for v in range(views)]
        )
    ]
    for copy in loads[:2] + loads[4:] + loads[2:4]:
        copy.start()

    barrier = pltpu.get_barrier_semaphore()

    def greet(tile, agent):
        pl.semaphore_signal(
            barrier, inc=1, device_id={"tile": tile, "agent": agent}, device_id_type=MESH
        )

    each(n_tile, lambda k: greet(lax.rem(me + k, n_tile), ag), 1)
    has_low, has_high = me > 0, me < n_tile - 1
    for k in range(1, n_agent):
        other = lax.rem(ag + k, n_agent)
        greet(me, other)

        @pl.when(has_low)
        def _():
            greet(me - 1, other)

        @pl.when(has_high)
        def _():
            greet(me + 1, other)

    loads[0].wait()
    start = [offsets_ref[0, v] // share for v in range(views)]
    local = [offsets_ref[0, v] - start[v] * share for v in range(views)]

    def choose(d):
        for j in range(pieces):
            found, shift = jnp.int32(views), jnp.int32(0)
            for v in range(views):
                hit = start[v] + j == d
                found = jnp.where(hit, v, found)
                shift = jnp.where(hit, local[v], shift)
            chosen[0, d * pieces + j] = found
            chosen[1, d * pieces + j] = shift

    each(n_tile, choose)
    placed[views] = jnp.zeros(form.placed_shape, jnp.float32)

    loads[1].wait()
    current = [states_ref[:, r, :] for r in range(height)]
    volume = jnp.concatenate(current, axis=1)
    volume_both = jnp.concatenate(split(volume), axis=0)
    for v in range(views):
        loads[4 + v].wait()
        fp_high[v * foot : (v + 1) * foot], fp_low[v * foot : (v + 1) * foot] = split(fp[v])

    def product(left, right):
        return lax.dot_general(
            left, right, (((1,), (1,)), ((), ())), preferred_element_type=jnp.float32
        )

    parts = product(fp_high[...], volume_both)
    extra = product(fp_low[...], volume_both)
    parts = jnp.transpose(parts + jnp.where(lanes(*extra.shape) < slices, extra, 0.0))
    projected = parts[:slices] + parts[slices:]
    for v in range(views):
        placed[v] = form.place(projected[:, v * foot : (v + 1) * foot], local[v])

    pl.semaphore_wait(
        barrier,
        n_tile - 1 + (n_agent - 1) * (1 + has_low.astype(jnp.int32) + has_high.astype(jnp.int32)),
    )

    def message(d):
        spots = [d * pieces + j for j in range(pieces)]
        return form.pack([chosen[0, i] for i in spots], [chosen[1, i] for i in spots], placed)

    def forward(d):
        return pltpu.make_async_remote_copy(
            src_ref=fsend.at[d], dst_ref=frecv.at[me], send_sem=fss.at[d], recv_sem=frs.at[me],
            device_id={"tile": d, "agent": ag}, device_id_type=MESH,
        )

    def forward_from(s):
        return pltpu.make_async_remote_copy(
            src_ref=fsend.at[s], dst_ref=frecv.at[s], send_sem=fss.at[s], recv_sem=frs.at[s],
            device_id={"tile": s, "agent": ag}, device_id_type=MESH,
        )

    def send_forward(k):
        d = lax.rem(me + k, n_tile)
        fsend[d] = message(d)
        forward(d).start()

    each(n_tile, send_forward, 1)
    frecv[me] = message(me)

    loads[2].wait()
    loads[3].wait()

    def add(sums, s):
        packed = frecv[s]
        for label, value in zip(form.labels(packed), form.values(packed)):
            sums = [old + jnp.where(label == v, value, 0.0) for v, old in enumerate(sums)]
        return tuple(sums)

    def gather(k, sums):
        s = lax.rem(me + n_tile - k, n_tile)
        forward_from(s).wait_recv()
        return add(sums, s)

    sums = add([-measured_ref[v] for v in range(views)], me)
    if n_tile <= 16:
        for k in reversed(far_first(n_tile)):
            sums = gather(k, sums)
    else:
        sums = lax.fori_loop(1, n_tile, gather, sums)
    residual = [weights_ref[v] * sums[v] for v in range(views)]

    def answer(s):
        values = []
        for label in form.labels(frecv[s]):
            value = jnp.zeros((slices, share), jnp.float32)
            for v in range(views):
                value = jnp.where(label == v, residual[v], value)
            values.append(value)
        return form.answer(values)

    def backward(d):
        return pltpu.make_async_remote_copy(
            src_ref=bsend.at[d], dst_ref=brecv.at[me], send_sem=bss.at[d], recv_sem=brs.at[me],
            device_id={"tile": d, "agent": ag}, device_id_type=MESH,
        )

    def backward_from(s):
        return pltpu.make_async_remote_copy(
            src_ref=bsend.at[s], dst_ref=brecv.at[s], send_sem=bss.at[s], recv_sem=brs.at[s],
            device_id={"tile": s, "agent": ag}, device_id_type=MESH,
        )

    def send_backward(k):
        d = lax.rem(me + k, n_tile)
        bsend[d] = answer(d)
        backward(d).start()

    each(n_tile, send_backward, 1)
    brecv[me] = answer(me)
    each(n_tile, lambda k: backward_from(lax.rem(me + n_tile - k, n_tile)).wait_recv(), 1)

    windows = [
        form.window(lambda j: brecv[jnp.minimum(start[v] + j, n_tile - 1)], local[v])
        for v in range(views)
    ]
    high, low = split(jnp.concatenate(windows, axis=1))
    both = jnp.dot(
        jnp.concatenate([high, low], axis=0), fp_high[...], preferred_element_type=jnp.float32
    )
    gradient = both[:slices] + both[slices:]
    gradient += jnp.dot(high, fp_low[...], preferred_element_type=jnp.float32)
    reflect = volume - (2.0 * STEP_SIZE) * gradient
    rsend[...] = reflect

    def share_copy(agent, step):
        return pltpu.make_async_remote_copy(
            src_ref=rsend, dst_ref=rrecv.at[ag, 1 - step],
            send_sem=rss.at[agent, 1 + step], recv_sem=rrs.at[ag, 1 - step],
            device_id={"tile": me + step, "agent": agent}, device_id_type=MESH,
        )

    def share_from(agent, step):
        return pltpu.make_async_remote_copy(
            src_ref=rsend, dst_ref=rrecv.at[agent, 1 + step],
            send_sem=rss.at[agent, 1 + step], recv_sem=rrs.at[agent, 1 + step],
            device_id={"tile": me + step, "agent": agent}, device_id_type=MESH,
        )

    def sharing(act):
        for k in range(1, n_agent):
            act(lax.rem(ag + k, n_agent), 0)
        for step, there in ((-1, has_low), (1, has_high)):

            @pl.when(there)
            def _():
                for k in range(n_agent):
                    act(lax.rem(ag + k, n_agent), step)

    sharing(lambda agent, step: share_copy(agent, step).start())
    rrecv[ag, 1] = reflect

    @pl.when(jnp.logical_not(has_low))
    def _():
        rrecv[:, 0] = jnp.zeros((n_agent, slices, pixels), jnp.float32)

    @pl.when(jnp.logical_not(has_high))
    def _():
        rrecv[:, 2] = jnp.zeros((n_agent, slices, pixels), jnp.float32)

    for r in range(height):
        mine = reflect[:, r * width : (r + 1) * width]
        base_ref[r] = (1.0 - RELAX) * current[r] - RELAX * mine

    each(n_tile, lambda k: forward(lax.rem(me + k, n_tile)).wait_send(), 1)
    each(n_tile, lambda k: backward(lax.rem(me + k, n_tile)).wait_send(), 1)
    sharing(lambda agent, step: share_from(agent, step).wait_recv())

    for spot in range(3):
        total = rrecv[0, spot]
        for a in range(1, n_agent):
            total = total + rrecv[a, spot]
        total = total * (1.0 / n_agent)
        for r in range(height):
            average_ref[spot * height + r] = total[:, r * width : (r + 1) * width]
    sharing(lambda agent, step: share_copy(agent, step).wait_send())


def prior_kernel(n_tile, average_ref, base_ref, new_ref, prior_ref):
    me = lax.axis_index("tile")
    height = base_ref.shape[0]
    reach = height - SWEEPS
    rows = [average_ref[i] for i in range(reach, 3 * height - reach)]
    low = jnp.where(me > 0, 1.0, 0.0)
    high = jnp.where(me < n_tile - 1, 1.0, 0.0)
    means = rows
    for sweep in range(SWEEPS):
        rows = sweep_rows(rows, means)
        means = means[1:-1]
        outer = SWEEPS - 1 - sweep
        rows = [
            row * low if i < outer else row * high if i >= len(rows) - outer else row
            for i, row in enumerate(rows)
        ]
    for r in range(height):
        prior_ref[:, r, :] = rows[r]
        new_ref[0, :, r, :] = base_ref[r] + (2.0 * RELAX) * rows[r]


def shards(n_tile, n_agent, states, footprints, offsets, measured, weights):
    _, slices, height, width = states.shape
    views, _, foot, pixels = footprints.shape
    share = measured.shape[2]
    fold = share == 2 * foot and share % 128 == 0
    form = (Folded if fold else Windows)(slices, views, foot, share)
    vmem = pl.BlockSpec(memory_space=pltpu.VMEM)
    hbm = pl.BlockSpec(memory_space=pltpu.HBM)
    f32 = jnp.float32
    dma = pltpu.SemaphoreType.DMA
    operands = states, footprints, offsets.reshape(1, views), measured, weights
    operands = [pltpu.with_memory_space_constraint(x, pltpu.HBM) for x in operands]
    average, base = pl.pallas_call(
        functools.partial(kernel, n_tile, n_agent, form),
        out_shape=(
            pltpu.VMEM((3 * height, slices, width), f32),
            pltpu.VMEM((height, slices, width), f32),
        ),
        in_specs=[hbm] * 5,
        out_specs=(vmem, vmem),
        scratch_shapes=[
            pltpu.VMEM((slices, height, width), f32),
            pltpu.VMEM((views, foot, pixels), f32),
            pltpu.SMEM((1, views), jnp.int32),
            pltpu.VMEM(measured.shape, f32),
            pltpu.VMEM(weights.shape, f32),
            pltpu.VMEM((views * foot, pixels), jnp.bfloat16),
            pltpu.VMEM((views * foot, pixels), jnp.bfloat16),
            pltpu.VMEM((views + 1,) + form.placed_shape, f32),
            pltpu.SMEM((2, n_tile * form.pieces), jnp.int32),
            pltpu.VMEM((n_tile, form.rows, share), f32),
            pltpu.VMEM((n_tile, form.rows, share), f32),
            pltpu.VMEM((n_tile,) + form.back_shape, f32),
            pltpu.VMEM((n_tile,) + form.back_shape, f32),
            pltpu.VMEM((slices, pixels), f32),
            pltpu.VMEM((n_agent, 3, slices, pixels), f32),
            dma((4 + views,)),
            dma((n_tile,)),
            dma((n_tile,)),
            dma((n_tile,)),
            dma((n_tile,)),
            dma((n_agent, 3)),
            dma((n_agent, 3)),
        ],
        compiler_params=pltpu.CompilerParams(
            collective_id=0, has_side_effects=True, vmem_limit_bytes=24 * 2**20
        ),
    )(*operands)
    return tuple(
        pl.pallas_call(
            functools.partial(prior_kernel, n_tile),
            out_shape=(
                jax.ShapeDtypeStruct(states.shape, f32),
                jax.ShapeDtypeStruct(states.shape[1:], f32),
            ),
            in_specs=[vmem, vmem],
            out_specs=(vmem, vmem),
            compiler_params=pltpu.CompilerParams(vmem_limit_bytes=24 * 2**20),
        )(average, base)
    )


def solution(mesh):
    in_specs = (
        P("agent", None, "tile", None),
        P("agent", "tile", None, None),
        P("agent", "tile"),
        P("agent", None, "tile"),
        P("agent", None, "tile"),
    )
    out_specs = (P("agent", None, "tile", None), P(None, "tile", None))
    body = functools.partial(shards, mesh.shape["tile"], mesh.shape["agent"])
    return jax.shard_map(body, mesh=mesh, in_specs=in_specs, out_specs=out_specs, check_vma=False)
```

```python
import functools

import jax
import jax.numpy as jnp
from jax import lax
from jax.experimental import pallas as pl
from jax.experimental.pallas import tpu as pltpu
from jax.sharding import PartitionSpec as P

SWEEPS = 2
STEP_SIZE = 0.25
RELAX = 0.6
QRATIO = 0.6
MESH = pl.DeviceIdType.MESH


def neighbour_table():
    offsets_nb = []
    for a in (-1, 0, 1):
        for b in (-1, 0, 1):
            for c in (-1, 0, 1):
                if a != 0 or b != 0 or c != 0:
                    offsets_nb.append((a, b, c, a * a + b * b + c * c))
    total = sum(1.0 / item[3] ** 0.5 for item in offsets_nb)
    scale = {n: 4.0 / n**0.5 / total for n in (1, 2, 3)}
    return offsets_nb, scale


def shift_zero(value, step, dim):
    if step == 0:
        return value
    size = value.shape[dim]
    index = lax.broadcasted_iota(jnp.int32, value.shape, dim)
    rolled = pltpu.roll(value, (-step) % size, dim)
    inside = index < size - 1 if step == 1 else index >= 1
    return jnp.where(inside, rolled, 0.0)


def sweep_rows(rows, averages):
    offsets_nb, scale = neighbour_table()
    shifted = [
        {(a, c): shift_zero(shift_zero(row, a, 0), c, 1) for a in (-1, 0, 1) for c in (-1, 0, 1)}
        for row in rows
    ]
    result = []
    for r in range(1, len(rows) - 1):
        centre = rows[r]
        num, den = {}, {}
        for a, b, c, kind in offsets_nb:
            neighbour = shifted[r + b][(a, c)]
            differ = centre - neighbour
            powered = jnp.exp(0.4 * jnp.log(differ * differ))
            inverse = pl.reciprocal(1.0 + powered, approx=True)
            coefficient = inverse * (QRATIO + (1.0 - QRATIO) * inverse)
            num[kind] = num[kind] + coefficient * neighbour if kind in num else coefficient * neighbour
            den[kind] = den[kind] + coefficient if kind in den else coefficient
        top = averages[r] + sum(scale[n] * num[n] for n in num)
        bottom = 1.0 + sum(scale[n] * den[n] for n in den)
        result.append(top / bottom)
    return result


GROUP = 5


def each(count, body, first=0):
    if count <= 16:
        for k in range(first, count):
            body(k)
    else:
        lax.fori_loop(first, count, lambda k, c: (body(k), c)[1], 0)


def split(value):
    high = value.astype(jnp.bfloat16)
    return high, (value - high.astype(jnp.float32)).astype(jnp.bfloat16)


def lanes(rows, count):
    return lax.broadcasted_iota(jnp.int32, (rows, count), 1)


class Windows:
    def __init__(self, slices, views, foot, share):
        self.slices, self.views, self.foot, self.share = slices, views, foot, share
        self.pieces = (2 * share + foot - 2) // share
        self.width = -(-self.pieces * share // 128) * 128
        self.rows = self.pieces * slices + self.pieces
        self.placed_shape = (self.pieces, slices, share)
        self.back_shape = (self.pieces * slices, share)

    def place(self, block, shift):
        zeros = jnp.zeros((self.slices, self.width - self.foot), jnp.float32)
        rolled = pltpu.roll(jnp.concatenate([block, zeros], axis=1), shift, 1)
        share = self.share
        return jnp.stack([rolled[:, j * share : (j + 1) * share] for j in range(self.pieces)])

    def pack(self, views, shifts, placed):
        parts = [placed[v, j] for j, v in enumerate(views)]
        parts += [jnp.full((1, self.share), v.astype(jnp.float32)) for v in views]
        return jnp.concatenate(parts, axis=0)

    def labels(self, packed):
        base = self.pieces * self.slices
        shape = (self.slices, self.share)
        return [jnp.broadcast_to(packed[base + j : base + j + 1], shape) for j in range(self.pieces)]

    def values(self, packed):
        return [packed[j * self.slices : (j + 1) * self.slices] for j in range(self.pieces)]

    def answer(self, values):
        return jnp.concatenate(values, axis=0)

    def window(self, load, shift):
        parts = [load(j)[j * self.slices : (j + 1) * self.slices] for j in range(self.pieces)]
        rest = self.width - self.pieces * self.share
        if rest:
            parts.append(jnp.zeros((self.slices, rest), jnp.float32))
        whole = jnp.concatenate(parts, axis=1)
        return pltpu.roll(whole, self.width - shift, 1)[:, : self.foot]


class Folded:
    pieces = 2

    def __init__(self, slices, views, foot, share):
        self.slices, self.views, self.foot, self.share = slices, views, foot, share
        self.rows = slices + 2
        self.placed_shape = (1, slices, share)
        self.back_shape = (slices, share)

    def halves(self):
        lane = lanes(self.slices, self.share)
        return lane, lane < self.foot

    def place(self, block, shift):
        lane, lower = self.halves()
        rolled = pltpu.roll(jnp.concatenate([block, block], axis=1), shift, 1)
        spill = shift - self.foot
        slack = jnp.where(lower, spill - 1 - lane, lane - self.foot - spill)
        return jnp.where(slack >= 0, rolled, 0.0)[None]

    def pack(self, views, shifts, placed):
        _, lower = self.halves()
        lane = lanes(1, self.share)
        body = jnp.where(lower, placed[views[1], 0], placed[views[0], 0])
        none = jnp.float32(self.views)
        first = (lane >= shifts[0]) & (lane < shifts[0] + self.foot)
        first = jnp.where(first, views[0].astype(jnp.float32), none)
        second = jnp.where(lane < shifts[1] - self.foot, views[1].astype(jnp.float32), none)
        return jnp.concatenate([body, first, second], axis=0)

    def labels(self, packed):
        shape = (self.slices, self.share)
        base = self.slices
        return [jnp.broadcast_to(packed[base + j : base + j + 1], shape) for j in range(2)]

    def values(self, packed):
        _, lower = self.halves()
        body = packed[: self.slices]
        return [jnp.where(lower, pltpu.roll(body, self.foot, 1), body), body]

    def answer(self, values):
        _, lower = self.halves()
        return jnp.where(lower, values[1], values[0] + pltpu.roll(values[0], self.foot, 1))

    def window(self, load, shift):
        lane, lower = self.halves()
        first, second = load(0), load(1)
        first = jnp.where(lower, pltpu.roll(first, self.foot, 1), first)
        second = jnp.where(lower, second, pltpu.roll(second, self.foot, 1))
        residue = jnp.where(lower, lane, lane - self.foot)
        both = jnp.where(residue < shift - self.foot, second, first)
        return pltpu.roll(both, self.share - shift, 1)[:, : self.foot]


def kernel(
    n_tile, n_agent, form, states_hbm, blocks_hbm, offsets_hbm, measured_hbm, weights_hbm,
    average_ref, base_ref,
    states_ref, fp, offsets_ref, measured_ref, weights_ref,
    fp_high, fp_low, placed, chosen, fsend, frecv, bsend, brecv, rsend, rrecv,
    load_sem, fss, frs, bss, brs, rss, rrs,
):
    me, ag = lax.axis_index("tile"), lax.axis_index("agent")
    slices, height, width = states_ref.shape
    views, foot, pixels = fp.shape
    share = measured_ref.shape[2]
    pieces = form.pieces

    loads = [
        pltpu.make_async_copy(source, target, load_sem.at[i])
        for i, (source, target) in enumerate(
            [
                (offsets_hbm, offsets_ref),
                (states_hbm.at[0], states_ref),
                (measured_hbm, measured_ref),
                (weights_hbm, weights_ref),
            ]
            + [(blocks_hbm.at[v, 0], fp.at[v]) for v in range(views)]
        )
    ]
    for copy in loads[:2] + loads[4:] + loads[2:4]:
        copy.start()

    barrier = pltpu.get_barrier_semaphore()

    def greet(tile, agent):
        pl.semaphore_signal(
            barrier, inc=1, device_id={"tile": tile, "agent": agent}, device_id_type=MESH
        )

    each(n_tile, lambda k: greet(lax.rem(me + k, n_tile), ag), 1)
    has_low, has_high = me > 0, me < n_tile - 1
    for k in range(1, n_agent):
        other = lax.rem(ag + k, n_agent)
        greet(me, other)

        @pl.when(has_low)
        def _():
            greet(me - 1, other)

        @pl.when(has_high)
        def _():
            greet(me + 1, other)

    loads[0].wait()
    start = [offsets_ref[0, v] // share for v in range(views)]
    local = [offsets_ref[0, v] - start[v] * share for v in range(views)]

    def choose(d):
        for j in range(pieces):
            found, shift = jnp.int32(views), jnp.int32(0)
            for v in range(views):
                hit = start[v] + j == d
                found = jnp.where(hit, v, found)
                shift = jnp.where(hit, local[v], shift)
            chosen[0, d * pieces + j] = found
            chosen[1, d * pieces + j] = shift

    each(n_tile, choose)
    placed[views] = jnp.zeros(form.placed_shape, jnp.float32)

    loads[1].wait()
    current = [states_ref[:, r, :] for r in range(height)]
    volume = jnp.concatenate(current, axis=1)
    volume_both = jnp.concatenate(split(volume), axis=0)
    for v in range(views):
        loads[4 + v].wait()
        fp_high[v * foot : (v + 1) * foot], fp_low[v * foot : (v + 1) * foot] = split(fp[v])

    def product(left, right):
        return lax.dot_general(
            left, right, (((1,), (1,)), ((), ())), preferred_element_type=jnp.float32
        )

    parts = product(fp_high[...], volume_both)
    extra = product(fp_low[...], volume_both)
    parts = jnp.transpose(parts + jnp.where(lanes(*extra.shape) < slices, extra, 0.0))
    projected = parts[:slices] + parts[slices:]
    for v in range(views):
        placed[v] = form.place(projected[:, v * foot : (v + 1) * foot], local[v])

    pl.semaphore_wait(
        barrier,
        n_tile - 1 + (n_agent - 1) * (1 + has_low.astype(jnp.int32) + has_high.astype(jnp.int32)),
    )

    def message(d):
        spots = [d * pieces + j for j in range(pieces)]
        return form.pack([chosen[0, i] for i in spots], [chosen[1, i] for i in spots], placed)

    def forward(d):
        return pltpu.make_async_remote_copy(
            src_ref=fsend.at[d], dst_ref=frecv.at[me], send_sem=fss.at[d], recv_sem=frs.at[me],
            device_id={"tile": d, "agent": ag}, device_id_type=MESH,
        )

    def forward_from(s):
        return pltpu.make_async_remote_copy(
            src_ref=fsend.at[s], dst_ref=frecv.at[s], send_sem=fss.at[s], recv_sem=frs.at[s],
            device_id={"tile": s, "agent": ag}, device_id_type=MESH,
        )

    def in_groups(prepare, act):
        if n_tile > 16:
            each(n_tile, lambda k: (prepare(k), act(k)), 1)
            return
        for low in range(1, n_tile, GROUP):
            group = range(low, min(low + GROUP, n_tile))
            for k in group:
                prepare(k)
            for k in group:
                act(k)

    def prepare_forward(k):
        d = lax.rem(me + k, n_tile)
        fsend[d] = message(d)

    in_groups(prepare_forward, lambda k: forward(lax.rem(me + k, n_tile)).start())
    frecv[me] = message(me)

    loads[2].wait()
    loads[3].wait()

    def add(sums, s):
        packed = frecv[s]
        for label, value in zip(form.labels(packed), form.values(packed)):
            sums = [old + jnp.where(label == v, value, 0.0) for v, old in enumerate(sums)]
        return tuple(sums)

    def arrive(k):
        s = lax.rem(me + n_tile - k, n_tile)
        forward_from(s).wait_recv()
        return s

    sums = add([-measured_ref[v] for v in range(views)], me)
    if n_tile <= 16:
        for low in range(1, n_tile, GROUP):
            for s in [arrive(k) for k in range(low, min(low + GROUP, n_tile))]:
                sums = add(sums, s)
    else:
        sums = lax.fori_loop(1, n_tile, lambda k, sums: add(sums, arrive(k)), sums)
    residual = [weights_ref[v] * sums[v] for v in range(views)]

    def answer(s):
        values = []
        for label in form.labels(frecv[s]):
            value = jnp.zeros((slices, share), jnp.float32)
            for v in range(views):
                value = jnp.where(label == v, residual[v], value)
            values.append(value)
        return form.answer(values)

    def backward(d):
        return pltpu.make_async_remote_copy(
            src_ref=bsend.at[d], dst_ref=brecv.at[me], send_sem=bss, recv_sem=brs,
            device_id={"tile": d, "agent": ag}, device_id_type=MESH,
        )

    def all_backward():
        count = pl.ds(0, n_tile - 1)
        return pltpu.make_async_remote_copy(
            src_ref=bsend.at[count], dst_ref=brecv.at[count], send_sem=bss, recv_sem=brs,
            device_id={"tile": lax.rem(me + 1, n_tile), "agent": ag}, device_id_type=MESH,
        )

    def prepare_backward(k):
        d = lax.rem(me + k, n_tile)
        bsend[d] = answer(d)

    in_groups(prepare_backward, lambda k: backward(lax.rem(me + k, n_tile)).start())
    brecv[me] = answer(me)
    all_backward().wait_recv()

    windows = [
        form.window(lambda j: brecv[jnp.minimum(start[v] + j, n_tile - 1)], local[v])
        for v in range(views)
    ]
    high, low = split(jnp.concatenate(windows, axis=1))
    both = jnp.dot(
        jnp.concatenate([high, low], axis=0), fp_high[...], preferred_element_type=jnp.float32
    )
    gradient = both[:slices] + both[slices:]
    gradient += jnp.dot(high, fp_low[...], preferred_element_type=jnp.float32)
    reflect = volume - (2.0 * STEP_SIZE) * gradient
    rsend[...] = reflect

    def share_copy(agent, step):
        return pltpu.make_async_remote_copy(
            src_ref=rsend, dst_ref=rrecv.at[ag, 1 - step],
            send_sem=rss.at[agent, 1 + step], recv_sem=rrs.at[ag, 1 - step],
            device_id={"tile": me + step, "agent": agent}, device_id_type=MESH,
        )

    def share_from(agent, step):
        return pltpu.make_async_remote_copy(
            src_ref=rsend, dst_ref=rrecv.at[agent, 1 + step],
            send_sem=rss.at[agent, 1 + step], recv_sem=rrs.at[agent, 1 + step],
            device_id={"tile": me + step, "agent": agent}, device_id_type=MESH,
        )

    def sharing(act):
        for k in range(1, n_agent):
            act(lax.rem(ag + k, n_agent), 0)
        for step, there in ((-1, has_low), (1, has_high)):

            @pl.when(there)
            def _():
                for k in range(n_agent):
                    act(lax.rem(ag + k, n_agent), step)

    sharing(lambda agent, step: share_copy(agent, step).start())
    rrecv[ag, 1] = reflect

    @pl.when(jnp.logical_not(has_low))
    def _():
        rrecv[:, 0] = jnp.zeros((n_agent, slices, pixels), jnp.float32)

    @pl.when(jnp.logical_not(has_high))
    def _():
        rrecv[:, 2] = jnp.zeros((n_agent, slices, pixels), jnp.float32)

    for r in range(height):
        mine = reflect[:, r * width : (r + 1) * width]
        base_ref[r] = (1.0 - RELAX) * current[r] - RELAX * mine

    each(n_tile, lambda k: forward(lax.rem(me + k, n_tile)).wait_send(), 1)
    all_backward().wait_send()
    sharing(lambda agent, step: share_from(agent, step).wait_recv())

    for spot in range(3):
        total = rrecv[0, spot]
        for a in range(1, n_agent):
            total = total + rrecv[a, spot]
        total = total * (1.0 / n_agent)
        for r in range(height):
            average_ref[spot * height + r] = total[:, r * width : (r + 1) * width]
    sharing(lambda agent, step: share_copy(agent, step).wait_send())


def prior_kernel(n_tile, average_ref, base_ref, new_ref, prior_ref):
    me = lax.axis_index("tile")
    height = base_ref.shape[0]
    reach = height - SWEEPS
    rows = [average_ref[i] for i in range(reach, 3 * height - reach)]
    low = jnp.where(me > 0, 1.0, 0.0)
    high = jnp.where(me < n_tile - 1, 1.0, 0.0)
    means = rows
    for sweep in range(SWEEPS):
        rows = sweep_rows(rows, means)
        means = means[1:-1]
        outer = SWEEPS - 1 - sweep
        rows = [
            row * low if i < outer else row * high if i >= len(rows) - outer else row
            for i, row in enumerate(rows)
        ]
    for r in range(height):
        prior_ref[:, r, :] = rows[r]
        new_ref[0, :, r, :] = base_ref[r] + (2.0 * RELAX) * rows[r]


def shards(n_tile, n_agent, states, footprints, offsets, measured, weights):
    _, slices, height, width = states.shape
    views, _, foot, pixels = footprints.shape
    share = measured.shape[2]
    fold = share == 2 * foot and share % 128 == 0
    form = (Folded if fold else Windows)(slices, views, foot, share)
    vmem = pl.BlockSpec(memory_space=pltpu.VMEM)
    hbm = pl.BlockSpec(memory_space=pltpu.HBM)
    f32 = jnp.float32
    dma = pltpu.SemaphoreType.DMA
    operands = states, footprints, offsets.reshape(1, views), measured, weights
    operands = [pltpu.with_memory_space_constraint(x, pltpu.HBM) for x in operands]
    average, base = pl.pallas_call(
        functools.partial(kernel, n_tile, n_agent, form),
        out_shape=(
            pltpu.VMEM((3 * height, slices, width), f32),
            pltpu.VMEM((height, slices, width), f32),
        ),
        in_specs=[hbm] * 5,
        out_specs=(vmem, vmem),
        scratch_shapes=[
            pltpu.VMEM((slices, height, width), f32),
            pltpu.VMEM((views, foot, pixels), f32),
            pltpu.SMEM((1, views), jnp.int32),
            pltpu.VMEM(measured.shape, f32),
            pltpu.VMEM(weights.shape, f32),
            pltpu.VMEM((views * foot, pixels), jnp.bfloat16),
            pltpu.VMEM((views * foot, pixels), jnp.bfloat16),
            pltpu.VMEM((views + 1,) + form.placed_shape, f32),
            pltpu.SMEM((2, n_tile * form.pieces), jnp.int32),
            pltpu.VMEM((n_tile, form.rows, share), f32),
            pltpu.VMEM((n_tile, form.rows, share), f32),
            pltpu.VMEM((n_tile,) + form.back_shape, f32),
            pltpu.VMEM((n_tile,) + form.back_shape, f32),
            pltpu.VMEM((slices, pixels), f32),
            pltpu.VMEM((n_agent, 3, slices, pixels), f32),
            dma((4 + views,)),
            dma((n_tile,)),
            dma((n_tile,)),
            dma,
            dma,
            dma((n_agent, 3)),
            dma((n_agent, 3)),
        ],
        compiler_params=pltpu.CompilerParams(
            collective_id=0, has_side_effects=True, vmem_limit_bytes=24 * 2**20
        ),
    )(*operands)
    return tuple(
        pl.pallas_call(
            functools.partial(prior_kernel, n_tile),
            out_shape=(
                jax.ShapeDtypeStruct(states.shape, f32),
                jax.ShapeDtypeStruct(states.shape[1:], f32),
            ),
            in_specs=[vmem, vmem],
            out_specs=(vmem, vmem),
            compiler_params=pltpu.CompilerParams(vmem_limit_bytes=24 * 2**20),
        )(average, base)
    )


def solution(mesh):
    in_specs = (
        P("agent", None, "tile", None),
        P("agent", "tile", None, None),
        P("agent", "tile"),
        P("agent", None, "tile"),
        P("agent", None, "tile"),
    )
    out_specs = (P("agent", None, "tile", None), P(None, "tile", None))
    body = functools.partial(shards, mesh.shape["tile"], mesh.shape["agent"])
    return jax.shard_map(body, mesh=mesh, in_specs=in_specs, out_specs=out_specs, check_vma=False)
```

```python
import functools

import jax
import jax.numpy as jnp
from jax import lax
from jax.experimental import pallas as pl
from jax.experimental.pallas import tpu as pltpu
from jax.sharding import PartitionSpec as P

SWEEPS = 2
STEP_SIZE = 0.25
RELAX = 0.6
QRATIO = 0.6
MESH = pl.DeviceIdType.MESH


def neighbour_table():
    offsets_nb = []
    for a in (-1, 0, 1):
        for b in (-1, 0, 1):
            for c in (-1, 0, 1):
                if a != 0 or b != 0 or c != 0:
                    offsets_nb.append((a, b, c, a * a + b * b + c * c))
    total = sum(1.0 / item[3] ** 0.5 for item in offsets_nb)
    scale = {n: 4.0 / n**0.5 / total for n in (1, 2, 3)}
    return offsets_nb, scale


def shift_zero(value, step, dim):
    if step == 0:
        return value
    size = value.shape[dim]
    index = lax.broadcasted_iota(jnp.int32, value.shape, dim)
    rolled = pltpu.roll(value, (-step) % size, dim)
    inside = index < size - 1 if step == 1 else index >= 1
    return jnp.where(inside, rolled, 0.0)


def sweep_rows(rows, averages):
    offsets_nb, scale = neighbour_table()
    shifted = [
        {(a, c): shift_zero(shift_zero(row, a, 0), c, 1) for a in (-1, 0, 1) for c in (-1, 0, 1)}
        for row in rows
    ]
    result = []
    for r in range(1, len(rows) - 1):
        centre = rows[r]
        num, den = {}, {}
        for a, b, c, kind in offsets_nb:
            neighbour = shifted[r + b][(a, c)]
            differ = centre - neighbour
            powered = jnp.exp(0.4 * jnp.log(differ * differ))
            inverse = pl.reciprocal(1.0 + powered, approx=True)
            coefficient = inverse * (QRATIO + (1.0 - QRATIO) * inverse)
            num[kind] = num[kind] + coefficient * neighbour if kind in num else coefficient * neighbour
            den[kind] = den[kind] + coefficient if kind in den else coefficient
        top = averages[r] + sum(scale[n] * num[n] for n in num)
        bottom = 1.0 + sum(scale[n] * den[n] for n in den)
        result.append(top / bottom)
    return result


GROUP = 5


def each(count, body, first=0):
    if count <= 16:
        for k in range(first, count):
            body(k)
    else:
        lax.fori_loop(first, count, lambda k, c: (body(k), c)[1], 0)


def split(value):
    high = value.astype(jnp.bfloat16)
    return high, (value - high.astype(jnp.float32)).astype(jnp.bfloat16)


def lanes(rows, count):
    return lax.broadcasted_iota(jnp.int32, (rows, count), 1)


class Windows:
    def __init__(self, slices, views, foot, share):
        self.slices, self.views, self.foot, self.share = slices, views, foot, share
        self.pieces = (2 * share + foot - 2) // share
        self.width = -(-self.pieces * share // 128) * 128
        self.rows = self.pieces * slices + self.pieces
        self.placed_shape = (self.pieces, slices, share)
        self.back_shape = (self.pieces * slices, share)

    def place(self, block, shift):
        zeros = jnp.zeros((self.slices, self.width - self.foot), jnp.float32)
        rolled = pltpu.roll(jnp.concatenate([block, zeros], axis=1), shift, 1)
        share = self.share
        return jnp.stack([rolled[:, j * share : (j + 1) * share] for j in range(self.pieces)])

    def pack(self, views, shifts, placed):
        parts = [placed[v, j] for j, v in enumerate(views)]
        parts += [jnp.full((1, self.share), v.astype(jnp.float32)) for v in views]
        return jnp.concatenate(parts, axis=0)

    def labels(self, packed):
        base = self.pieces * self.slices
        shape = (self.slices, self.share)
        return [jnp.broadcast_to(packed[base + j : base + j + 1], shape) for j in range(self.pieces)]

    def values(self, packed):
        return [packed[j * self.slices : (j + 1) * self.slices] for j in range(self.pieces)]

    def answer(self, values):
        return jnp.concatenate(values, axis=0)

    def window(self, load, shift):
        parts = [load(j)[j * self.slices : (j + 1) * self.slices] for j in range(self.pieces)]
        rest = self.width - self.pieces * self.share
        if rest:
            parts.append(jnp.zeros((self.slices, rest), jnp.float32))
        whole = jnp.concatenate(parts, axis=1)
        return pltpu.roll(whole, self.width - shift, 1)[:, : self.foot]


class Folded:
    pieces = 2

    def __init__(self, slices, views, foot, share):
        self.slices, self.views, self.foot, self.share = slices, views, foot, share
        self.rows = slices + 2
        self.placed_shape = (1, slices, share)
        self.back_shape = (slices, share)

    def halves(self):
        lane = lanes(self.slices, self.share)
        return lane, lane < self.foot

    def place(self, block, shift):
        lane, lower = self.halves()
        rolled = pltpu.roll(jnp.concatenate([block, block], axis=1), shift, 1)
        spill = shift - self.foot
        slack = jnp.where(lower, spill - 1 - lane, lane - self.foot - spill)
        return jnp.where(slack >= 0, rolled, 0.0)[None]

    def pack(self, views, shifts, placed):
        _, lower = self.halves()
        lane = lanes(1, self.share)
        body = jnp.where(lower, placed[views[1], 0], placed[views[0], 0])
        none = jnp.float32(self.views)
        first = (lane >= shifts[0]) & (lane < shifts[0] + self.foot)
        first = jnp.where(first, views[0].astype(jnp.float32), none)
        second = jnp.where(lane < shifts[1] - self.foot, views[1].astype(jnp.float32), none)
        return jnp.concatenate([body, first, second], axis=0)

    def labels(self, packed):
        shape = (self.slices, self.share)
        base = self.slices
        return [jnp.broadcast_to(packed[base + j : base + j + 1], shape) for j in range(2)]

    def values(self, packed):
        _, lower = self.halves()
        body = packed[: self.slices]
        return [jnp.where(lower, pltpu.roll(body, self.foot, 1), body), body]

    def answer(self, values):
        _, lower = self.halves()
        return jnp.where(lower, values[1], values[0] + pltpu.roll(values[0], self.foot, 1))

    def window(self, load, shift):
        lane, lower = self.halves()
        first, second = load(0), load(1)
        first = jnp.where(lower, pltpu.roll(first, self.foot, 1), first)
        second = jnp.where(lower, second, pltpu.roll(second, self.foot, 1))
        residue = jnp.where(lower, lane, lane - self.foot)
        both = jnp.where(residue < shift - self.foot, second, first)
        return pltpu.roll(both, self.share - shift, 1)[:, : self.foot]


def kernel(
    n_tile, n_agent, form, states_hbm, blocks_hbm, offsets_hbm, measured_hbm, weights_hbm,
    average_ref, base_ref,
    states_ref, fp, offsets_ref, measured_ref, weights_ref,
    fp_high, fp_low, placed, chosen, fsend, frecv, bsend, brecv, rsend, rrecv,
    load_sem, fss, frs, bss, brs, rss, rrs,
):
    me, ag = lax.axis_index("tile"), lax.axis_index("agent")
    slices, height, width = states_ref.shape
    views, foot, pixels = fp.shape
    share = measured_ref.shape[2]
    pieces = form.pieces

    loads = [
        pltpu.make_async_copy(source, target, load_sem.at[i])
        for i, (source, target) in enumerate(
            [
                (offsets_hbm, offsets_ref),
                (states_hbm.at[0], states_ref),
                (measured_hbm, measured_ref),
                (weights_hbm, weights_ref),
            ]
            + [(blocks_hbm.at[v, 0], fp.at[v]) for v in range(views)]
        )
    ]
    for copy in loads[:2] + loads[4:] + loads[2:4]:
        copy.start()

    barrier = pltpu.get_barrier_semaphore()

    def greet(tile, agent):
        pl.semaphore_signal(
            barrier, inc=1, device_id={"tile": tile, "agent": agent}, device_id_type=MESH
        )

    each(n_tile, lambda k: greet(lax.rem(me + k, n_tile), ag), 1)
    has_low, has_high = me > 0, me < n_tile - 1
    for k in range(1, n_agent):
        other = lax.rem(ag + k, n_agent)
        greet(me, other)

        @pl.when(has_low)
        def _():
            greet(me - 1, other)

        @pl.when(has_high)
        def _():
            greet(me + 1, other)

    loads[0].wait()
    start = [offsets_ref[0, v] // share for v in range(views)]
    local = [offsets_ref[0, v] - start[v] * share for v in range(views)]

    def choose(d):
        for j in range(pieces):
            found, shift = jnp.int32(views), jnp.int32(0)
            for v in range(views):
                hit = start[v] + j == d
                found = jnp.where(hit, v, found)
                shift = jnp.where(hit, local[v], shift)
            chosen[0, d * pieces + j] = found
            chosen[1, d * pieces + j] = shift

    each(n_tile, choose)
    placed[views] = jnp.zeros(form.placed_shape, jnp.float32)

    loads[1].wait()
    current = [states_ref[:, r, :] for r in range(height)]
    volume = jnp.concatenate(current, axis=1)
    volume_both = jnp.concatenate(split(volume), axis=0)
    def product(left, right):
        return lax.dot_general(
            left, right, (((1,), (1,)), ((), ())), preferred_element_type=jnp.float32
        )

    together = max(1, 128 // foot)
    for first in range(0, views, together):
        some = range(first, min(first + together, views))
        for v in some:
            loads[4 + v].wait()
            rows = slice(v * foot, (v + 1) * foot)
            fp_high[rows], fp_low[rows] = split(fp[v])
        rows = slice(first * foot, (some[-1] + 1) * foot)
        parts = product(fp_high[rows], volume_both)
        extra = product(fp_low[rows], volume_both)
        parts = jnp.transpose(parts + jnp.where(lanes(*extra.shape) < slices, extra, 0.0))
        projected = parts[:slices] + parts[slices:]
        for i, v in enumerate(some):
            placed[v] = form.place(projected[:, i * foot : (i + 1) * foot], local[v])

    def message(d):
        spots = [d * pieces + j for j in range(pieces)]
        return form.pack([chosen[0, i] for i in spots], [chosen[1, i] for i in spots], placed)

    def forward(d):
        return pltpu.make_async_remote_copy(
            src_ref=fsend.at[d], dst_ref=frecv.at[me], send_sem=fss.at[d], recv_sem=frs.at[me],
            device_id={"tile": d, "agent": ag}, device_id_type=MESH,
        )

    def forward_from(s):
        return pltpu.make_async_remote_copy(
            src_ref=fsend.at[s], dst_ref=frecv.at[s], send_sem=fss.at[s], recv_sem=frs.at[s],
            device_id={"tile": s, "agent": ag}, device_id_type=MESH,
        )

    def in_groups(prepare, act):
        if n_tile > 16:
            each(n_tile, lambda k: (prepare(k), act(k)), 1)
            return
        for low in range(1, n_tile, GROUP):
            group = range(low, min(low + GROUP, n_tile))
            for k in group:
                prepare(k)
            for k in group:
                act(k)

    def prepare_forward(k):
        d = lax.rem(me + k, n_tile)
        fsend[d] = message(d)

    each(n_tile, prepare_forward, 1)
    pl.semaphore_wait(
        barrier,
        n_tile - 1 + (n_agent - 1) * (1 + has_low.astype(jnp.int32) + has_high.astype(jnp.int32)),
    )
    each(n_tile, lambda k: forward(lax.rem(me + k, n_tile)).start(), 1)
    frecv[me] = message(me)

    loads[2].wait()
    loads[3].wait()

    def add(sums, s):
        packed = frecv[s]
        for label, value in zip(form.labels(packed), form.values(packed)):
            sums = [old + jnp.where(label == v, value, 0.0) for v, old in enumerate(sums)]
        return tuple(sums)

    def arrive(k):
        s = lax.rem(me + n_tile - k, n_tile)
        forward_from(s).wait_recv()
        return s

    sums = add([-measured_ref[v] for v in range(views)], me)
    if n_tile <= 16:
        for low in range(1, n_tile, GROUP):
            for s in [arrive(k) for k in range(low, min(low + GROUP, n_tile))]:
                sums = add(sums, s)
    else:
        sums = lax.fori_loop(1, n_tile, lambda k, sums: add(sums, arrive(k)), sums)
    residual = [weights_ref[v] * sums[v] for v in range(views)]

    def answer(s):
        values = []
        for label in form.labels(frecv[s]):
            value = jnp.zeros((slices, share), jnp.float32)
            for v in range(views):
                value = jnp.where(label == v, residual[v], value)
            values.append(value)
        return form.answer(values)

    def backward(d):
        return pltpu.make_async_remote_copy(
            src_ref=bsend.at[d], dst_ref=brecv.at[me], send_sem=bss, recv_sem=brs,
            device_id={"tile": d, "agent": ag}, device_id_type=MESH,
        )

    def all_backward():
        count = pl.ds(0, n_tile - 1)
        return pltpu.make_async_remote_copy(
            src_ref=bsend.at[count], dst_ref=brecv.at[count], send_sem=bss, recv_sem=brs,
            device_id={"tile": lax.rem(me + 1, n_tile), "agent": ag}, device_id_type=MESH,
        )

    def prepare_backward(k):
        d = lax.rem(me + k, n_tile)
        bsend[d] = answer(d)

    in_groups(prepare_backward, lambda k: backward(lax.rem(me + k, n_tile)).start())
    brecv[me] = answer(me)
    all_backward().wait_recv()

    windows = [
        form.window(lambda j: brecv[jnp.minimum(start[v] + j, n_tile - 1)], local[v])
        for v in range(views)
    ]
    high, low = split(jnp.concatenate(windows, axis=1))
    both = jnp.dot(
        jnp.concatenate([high, low], axis=0), fp_high[...], preferred_element_type=jnp.float32
    )
    gradient = both[:slices] + both[slices:]
    gradient += jnp.dot(high, fp_low[...], preferred_element_type=jnp.float32)
    reflect = volume - (2.0 * STEP_SIZE) * gradient
    rsend[...] = reflect

    def share_copy(agent, step):
        return pltpu.make_async_remote_copy(
            src_ref=rsend, dst_ref=rrecv.at[ag, 1 - step],
            send_sem=rss.at[agent, 1 + step], recv_sem=rrs.at[ag, 1 - step],
            device_id={"tile": me + step, "agent": agent}, device_id_type=MESH,
        )

    def share_from(agent, step):
        return pltpu.make_async_remote_copy(
            src_ref=rsend, dst_ref=rrecv.at[agent, 1 + step],
            send_sem=rss.at[agent, 1 + step], recv_sem=rrs.at[agent, 1 + step],
            device_id={"tile": me + step, "agent": agent}, device_id_type=MESH,
        )

    def sharing(act):
        for k in range(1, n_agent):
            act(lax.rem(ag + k, n_agent), 0)
        for step, there in ((-1, has_low), (1, has_high)):

            @pl.when(there)
            def _():
                for k in range(n_agent):
                    act(lax.rem(ag + k, n_agent), step)

    sharing(lambda agent, step: share_copy(agent, step).start())
    rrecv[ag, 1] = reflect

    @pl.when(jnp.logical_not(has_low))
    def _():
        rrecv[:, 0] = jnp.zeros((n_agent, slices, pixels), jnp.float32)

    @pl.when(jnp.logical_not(has_high))
    def _():
        rrecv[:, 2] = jnp.zeros((n_agent, slices, pixels), jnp.float32)

    for r in range(height):
        mine = reflect[:, r * width : (r + 1) * width]
        base_ref[r] = (1.0 - RELAX) * current[r] - RELAX * mine

    each(n_tile, lambda k: forward(lax.rem(me + k, n_tile)).wait_send(), 1)
    all_backward().wait_send()
    sharing(lambda agent, step: share_from(agent, step).wait_recv())

    for spot in range(3):
        total = rrecv[0, spot]
        for a in range(1, n_agent):
            total = total + rrecv[a, spot]
        total = total * (1.0 / n_agent)
        for r in range(height):
            average_ref[spot * height + r] = total[:, r * width : (r + 1) * width]
    sharing(lambda agent, step: share_copy(agent, step).wait_send())


def prior_kernel(n_tile, average_ref, base_ref, new_ref, prior_ref):
    me = lax.axis_index("tile")
    height = base_ref.shape[0]
    reach = height - SWEEPS
    rows = [average_ref[i] for i in range(reach, 3 * height - reach)]
    low = jnp.where(me > 0, 1.0, 0.0)
    high = jnp.where(me < n_tile - 1, 1.0, 0.0)
    means = rows
    for sweep in range(SWEEPS):
        rows = sweep_rows(rows, means)
        means = means[1:-1]
        outer = SWEEPS - 1 - sweep
        rows = [
            row * low if i < outer else row * high if i >= len(rows) - outer else row
            for i, row in enumerate(rows)
        ]
    for r in range(height):
        prior_ref[:, r, :] = rows[r]
        new_ref[0, :, r, :] = base_ref[r] + (2.0 * RELAX) * rows[r]


def shards(n_tile, n_agent, states, footprints, offsets, measured, weights):
    _, slices, height, width = states.shape
    views, _, foot, pixels = footprints.shape
    share = measured.shape[2]
    fold = share == 2 * foot and share % 128 == 0
    form = (Folded if fold else Windows)(slices, views, foot, share)
    vmem = pl.BlockSpec(memory_space=pltpu.VMEM)
    hbm = pl.BlockSpec(memory_space=pltpu.HBM)
    f32 = jnp.float32
    dma = pltpu.SemaphoreType.DMA
    operands = states, footprints, offsets.reshape(1, views), measured, weights
    operands = [pltpu.with_memory_space_constraint(x, pltpu.HBM) for x in operands]
    average, base = pl.pallas_call(
        functools.partial(kernel, n_tile, n_agent, form),
        out_shape=(
            pltpu.VMEM((3 * height, slices, width), f32),
            pltpu.VMEM((height, slices, width), f32),
        ),
        in_specs=[hbm] * 5,
        out_specs=(vmem, vmem),
        scratch_shapes=[
            pltpu.VMEM((slices, height, width), f32),
            pltpu.VMEM((views, foot, pixels), f32),
            pltpu.SMEM((1, views), jnp.int32),
            pltpu.VMEM(measured.shape, f32),
            pltpu.VMEM(weights.shape, f32),
            pltpu.VMEM((views * foot, pixels), jnp.bfloat16),
            pltpu.VMEM((views * foot, pixels), jnp.bfloat16),
            pltpu.VMEM((views + 1,) + form.placed_shape, f32),
            pltpu.SMEM((2, n_tile * form.pieces), jnp.int32),
            pltpu.VMEM((n_tile, form.rows, share), f32),
            pltpu.VMEM((n_tile, form.rows, share), f32),
            pltpu.VMEM((n_tile,) + form.back_shape, f32),
            pltpu.VMEM((n_tile,) + form.back_shape, f32),
            pltpu.VMEM((slices, pixels), f32),
            pltpu.VMEM((n_agent, 3, slices, pixels), f32),
            dma((4 + views,)),
            dma((n_tile,)),
            dma((n_tile,)),
            dma,
            dma,
            dma((n_agent, 3)),
            dma((n_agent, 3)),
        ],
        compiler_params=pltpu.CompilerParams(
            collective_id=0, has_side_effects=True, vmem_limit_bytes=24 * 2**20
        ),
    )(*operands)
    return tuple(
        pl.pallas_call(
            functools.partial(prior_kernel, n_tile),
            out_shape=(
                jax.ShapeDtypeStruct(states.shape, f32),
                jax.ShapeDtypeStruct(states.shape[1:], f32),
            ),
            in_specs=[vmem, vmem],
            out_specs=(vmem, vmem),
            compiler_params=pltpu.CompilerParams(vmem_limit_bytes=24 * 2**20),
        )(average, base)
    )


def solution(mesh):
    in_specs = (
        P("agent", None, "tile", None),
        P("agent", "tile", None, None),
        P("agent", "tile"),
        P("agent", None, "tile"),
        P("agent", None, "tile"),
    )
    out_specs = (P("agent", None, "tile", None), P(None, "tile", None))
    body = functools.partial(shards, mesh.shape["tile"], mesh.shape["agent"])
    return jax.shard_map(body, mesh=mesh, in_specs=in_specs, out_specs=out_specs, check_vma=False)
```
